32 devices in a mesh: gx: 4 (over x, core), yz: 8 (over z, y).
Axes of the slice: x: 2, y: 2, z: 4, core: 2. Of those that a mesh axis runs over, the one named last changes fastest.
Arguments:
- hidden_in: bfloat16 [128, 12288], P('gx', 'yz'), may hold values from -2000 to 2000
- norm_gain: float32 [12288], P('yz'), may hold values from 0.1 to 1.9
- query_key_value_weight: bfloat16 [12288, 8, 1792], P('yz', 'gx'), may hold values from -0.0546875 to 0.0546875
- out_weight: bfloat16 [12288, 12288], P('gx', 'yz'), may hold values from -0.21875 to 0.21875
- key_cache: bfloat16 [128, 2048, 8, 128], P('yz', None, 'gx'), may hold values from -404 to 404
- cached_value_rows: bfloat16 [128, 2048, 8, 128], P('yz', None, 'gx'), may hold values from -6 to 6
- lengths: int32 [128], P('yz'), may hold values from 4 to 2048, as said below
Outputs:
- attn_out: bfloat16 [128, 12288], P('gx', 'yz')
The draws below stay inside these ranges and needn't reach their ends.
Inputs may be any that keep to these rules, and one draw needn't show every extreme that they name: Row r's cache slots 0 to lengths[r] - 1 hold its tokens; the others are unused. Some row has 2048 cached tokens and some row has 4.
All inputs are finite; a program needn't handle non-finite values.
Results may differ from the reference program's by a relative error of at most 0.012.
The reference program's roundings to bfloat16 on the way (of `normed`, `probs` and `heads`) count: a program that leaves them out, or rounds other values in their place, can miss the bound.
Values may be sent and summed in bfloat16 or wider, within the bound.
A program may use at most 192 MiB of HBM per device.

```python
import math
import jax
import jax.numpy as jnp
from jax import lax

MODEL_WIDTH = 12288
HQ = 96
KEY_HEADS = 8
HEAD_SIZE = 128
CACHE_SLOTS = 2048
QUERIES_PER_KEY = 12
GROUP_COLUMNS = 1792
DECODED_ROWS = 128


def draw_hidden_in(key, part):
    key = jax.random.fold_in(key, 11)
    first, second_part, third_part = jax.random.split(key, 3)
    ramp = 1.0 + 2.0 * jnp.arange(MODEL_WIDTH, dtype=jnp.float32) / (MODEL_WIDTH - 1)
    column_scale = jnp.exp(jax.random.uniform(third_part, (1, MODEL_WIDTH), jnp.float32) * math.log(10.0)) * ramp[None, :]
    base = jnp.clip(jax.random.normal(first, (DECODED_ROWS, MODEL_WIDTH), jnp.float32), -5.0, 5.0)
    row_scale = jnp.exp(jax.random.uniform(second_part, (DECODED_ROWS, 1), jnp.float32) * math.log(10.0))
    return (base * row_scale * column_scale).astype(jnp.bfloat16)


def draw_key_cache(key, part):
    key = jax.random.fold_in(key, 13)
    first = jax.random.fold_in(key, 0)
    shape_tuple = (DECODED_ROWS, CACHE_SLOTS, KEY_HEADS, HEAD_SIZE)
    values = jnp.clip(1.5 * jax.random.normal(first, shape_tuple, jnp.float32), -9.0, 9.0)
    return values.astype(jnp.bfloat16)


def draw_lengths(key, part):
    key = jax.random.fold_in(key, 17)
    first, second_part, third_part = jax.random.split(key, 3)
    drawn = jax.random.randint(first, (DECODED_ROWS,), 4, CACHE_SLOTS + 1)
    longest = jax.random.randint(second_part, (), 0, DECODED_ROWS)
    shortest = (longest + 1 + jax.random.randint(third_part, (), 0, DECODED_ROWS - 1)) % DECODED_ROWS
    drawn = drawn.at[longest].set(CACHE_SLOTS)
    drawn = drawn.at[shortest].set(4)
    return drawn.astype(jnp.int32)


def level_of(key, dims, cuts, low, high):
    factor_of, own = 1.0, jax.random.fold_in(key, 6)
    for dim, blocks in cuts:
        draws = jnp.exp(jax.random.uniform(jax.random.fold_in(own, dim), (blocks,), jnp.float32, low / len(cuts), high / len(cuts)))
        factor_of = factor_of * jnp.repeat(draws, dims[dim] // blocks).reshape([-1 if axis == dim else 1 for axis in range(len(dims))])
    return factor_of


def normal_values(rng, shape, scale, reach, shards=(), kind=jnp.bfloat16):
    values = jax.random.normal(rng, shape, jnp.float32) * scale
    if len(shards) > 0:
        values = level_of(rng, shape, shards, -0.22, 0.18) * values
    return jnp.clip(values, min=-reach, max=reach).astype(kind)


def setup_inputs(seed: int = 0) -> dict:
    splits = jax.random.split(jax.random.key(seed), 8)
    return {
        "hidden_in": draw_hidden_in(jax.random.fold_in(splits[7], 71), 0),
        "norm_gain": jnp.clip(1.0 + 0.18 * jax.random.normal(splits[1], (MODEL_WIDTH,), jnp.float32), 0.1, 1.9),
        "query_key_value_weight": normal_values(splits[2], (MODEL_WIDTH, KEY_HEADS, GROUP_COLUMNS), MODEL_WIDTH ** -0.5, 0.0546875, ((0, 8), (1, 4))),
        "out_weight": normal_values(splits[3], (HQ * HEAD_SIZE, MODEL_WIDTH), (MODEL_WIDTH // 16) ** -0.5, 0.21875, ((0, 4), (1, 8))),
        "key_cache": draw_key_cache(jax.random.fold_in(splits[7], 71), 0),
        "cached_value_rows": normal_values(splits[5], (DECODED_ROWS, CACHE_SLOTS, KEY_HEADS, HEAD_SIZE), 1.0, 6.0, ((0, 8), (2, 4))),
        "lengths": draw_lengths(jax.random.fold_in(splits[7], 71), 0),
    }


EPS = 1e-05
ROPE_BASE = 1000000.0

def rotate(block, positions):
    half_width = block.shape[-1] // 2
    frequency = ROPE_BASE ** (-(jnp.arange(half_width, dtype=jnp.float32) * 2.0) / block.shape[-1])
    angles = positions[..., None] * frequency
    cosine = jnp.cos(angles)
    sine = jnp.sin(angles)
    first = block[..., :half_width]
    second_part = block[..., half_width:]
    return jnp.concatenate([first * cosine - second_part * sine, second_part * cosine + first * sine], axis=-1)

def reference(hidden_in, norm_gain, query_key_value_weight, out_weight, key_cache, cached_value_rows, lengths):
    inputs = hidden_in.astype(jnp.float32)
    squares = lax.optimization_barrier(jnp.sum(inputs * inputs, axis=1))
    normed = (inputs * lax.rsqrt(squares[:, None] / MODEL_WIDTH + EPS) * norm_gain).astype(jnp.bfloat16)
    weight_flat_matrix = query_key_value_weight.reshape(MODEL_WIDTH, KEY_HEADS * GROUP_COLUMNS)
    projected_rows = jnp.dot(normed, weight_flat_matrix, preferred_element_type=jnp.float32)
    projected_rows = projected_rows.reshape(DECODED_ROWS, KEY_HEADS, QUERIES_PER_KEY + 2, HEAD_SIZE)
    positions = lengths.astype(jnp.float32)
    queries = rotate(projected_rows[:, :, :QUERIES_PER_KEY], positions[:, None, None]).astype(jnp.bfloat16)
    new_keys = rotate(projected_rows[:, :, QUERIES_PER_KEY], positions[:, None]).astype(jnp.bfloat16)
    new_values = projected_rows[:, :, QUERIES_PER_KEY + 1].astype(jnp.bfloat16)
    factor = HEAD_SIZE ** (-0.5)
    valid = jnp.arange(CACHE_SLOTS, dtype=jnp.int32)[None, :] < lengths[:, None]

    def single_head(head):
        keys_head = lax.dynamic_index_in_dim(key_cache, head, 2, keepdims=False).astype(jnp.float32)
        values_head = lax.dynamic_index_in_dim(cached_value_rows, head, 2, keepdims=False).astype(jnp.float32)
        query_head = lax.dynamic_index_in_dim(queries, head, 1, keepdims=False).astype(jnp.float32)
        own_key = lax.dynamic_index_in_dim(new_keys, head, 1, keepdims=False).astype(jnp.float32)
        own_value = lax.dynamic_index_in_dim(new_values, head, 1, keepdims=False).astype(jnp.float32)
        scores = jnp.einsum('rgd,rjd->rgj', query_head, keys_head) * factor
        scores = jnp.where(valid[:, None, :], scores, -jnp.inf)
        own_score = jnp.einsum('rgd,rd->rg', query_head, own_key) * factor
        largest = jnp.maximum(lax.optimization_barrier(jnp.max(scores, axis=-1)), own_score)
        weights = jnp.exp(scores - largest[..., None])
        own_weight = jnp.exp(own_score - largest)
        totals = lax.optimization_barrier(jnp.sum(weights, axis=-1)) + own_weight
        probs = lax.optimization_barrier((weights / totals[..., None]).astype(jnp.bfloat16)).astype(jnp.float32)
        own_prob = lax.optimization_barrier((own_weight / totals).astype(jnp.bfloat16)).astype(jnp.float32)
        mixed = jnp.einsum('rgj,rjd->rgd', probs, values_head) + own_prob[..., None] * own_value[:, None, :]
        return mixed.astype(jnp.bfloat16)
    stacked_parts = lax.map(single_head, jnp.arange(KEY_HEADS, dtype=jnp.int32))
    heads = jnp.transpose(stacked_parts, (1, 0, 2, 3)).reshape(DECODED_ROWS, HQ * HEAD_SIZE)
    return jnp.dot(heads, out_weight, preferred_element_type=jnp.float32).astype(jnp.bfloat16)
```

```python
import functools

import jax
import jax.numpy as jnp
from jax import lax
from jax.experimental import pallas as pl
from jax.experimental.pallas import tpu as pltpu
from jax.sharding import PartitionSpec as P

HEAD_SIZE = 128
QUERIES_PER_KEY = 12
SLOTS = QUERIES_PER_KEY + 2

EPS = 1e-05
ROPE_BASE = 1000000.0
MESH = pl.DeviceIdType.MESH
VMEM = pl.BlockSpec(memory_space=pltpu.VMEM)
ANY = pl.BlockSpec(memory_space=pl.ANY)


def factors(n):
    inner = 1 << ((n.bit_length() - 1) // 2)
    return n // inner, inner


def greet(peers):
    barrier = pltpu.get_barrier_semaphore()
    for axis, index in peers:
        pl.semaphore_signal(barrier, inc=1, device_id={axis: index}, device_id_type=MESH)
    pl.semaphore_wait(barrier, len(peers))


def start_copy(src, dst, send_sem, recv_sem, axis, index):
    copy = pltpu.make_async_remote_copy(
        src_ref=src,
        dst_ref=dst,
        send_sem=send_sem,
        recv_sem=recv_sem,
        device_id={axis: index},
        device_id_type=MESH,
    )
    copy.start()
    return copy


def project_kernel(
    gx, yz, chunks,
    hidden_ref, gain_ref, weight_ref, out_ref,
    hid, squares, squares_in, normed, partial, inner_in, mid, outer_in,
    hid_send, hid_recv, sq_send, sq_recv, inner_send, inner_recv, outer_send, outer_recv,
):
    outer, inner = factors(yz)
    g = lax.axis_index("gx")
    i = lax.axis_index("yz")
    a = i // inner
    b = lax.rem(i, inner)
    greet(
        [("gx", lax.rem(g + d, gx)) for d in range(1, gx)]
        + [("yz", lax.rem(i + d, yz)) for d in range(1, yz)]
    )
    copies = []
    for d in range(1, gx):
        copies.append(
            start_copy(hidden_ref, hid.at[g], hid_send.at[d - 1], hid_recv.at[d - 1], "gx", lax.rem(g + d, gx))
        )
    hid[g] = hidden_ref[...]
    for copy in copies:
        copy.wait_recv()
    rows_each, depth = hidden_ref.shape
    rows = rows_each * gx
    x = hid[...].reshape(rows, depth).astype(jnp.float32)
    own = jnp.sum(x * x, axis=1, keepdims=True)
    squares[...] = jnp.broadcast_to(own, (rows, 128)).T[:8]
    sq_copies = []
    for d in range(1, yz):
        sq_copies.append(
            start_copy(squares, squares_in.at[d - 1], sq_send.at[d - 1], sq_recv.at[d - 1], "yz", lax.rem(i + d, yz))
        )
    total = squares[...]
    for d in range(1, yz):
        sq_copies[d - 1].wait_recv()
        total = total + squares_in[d - 1]
    column = jnp.broadcast_to(total[:1], (128, rows)).T[:, :1]
    scale = lax.rsqrt(column / (depth * yz) + EPS)
    normed[...] = (x * scale * gain_ref[...]).astype(jnp.bfloat16)
    copies += sq_copies

    kv = weight_ref.shape[0]
    per = chunks // kv
    width = weight_ref.shape[2] // per
    own_rows = rows // yz
    inner_copies, outer_copies = [], []

    def first(c):
        part = jnp.dot(
            normed[...],
            weight_ref[c // per, :, (c % per) * width : (c % per + 1) * width],
            preferred_element_type=jnp.float32,
        )
        for q in range(outer):
            for p in range(inner):
                start = (q * inner + p) * own_rows
                partial[c, p, q] = part[start : start + own_rows]
        here = []
        for d in range(1, inner):
            p = lax.rem(b + d, inner)
            here.append(
                start_copy(
                    partial.at[c, p], inner_in.at[c, d - 1], inner_send.at[c, d - 1], inner_recv.at[c, d - 1],
                    "yz", a * inner + p,
                )
            )
        inner_copies.append(here)

    def second(c):
        value = partial[c, b]
        for d in range(1, inner):
            inner_copies[c][d - 1].wait_recv()
            value = value + inner_in[c, d - 1]
        mid[c] = value
        here = []
        for d in range(1, outer):
            q = lax.rem(a + d, outer)
            here.append(
                start_copy(
                    mid.at[c, q], outer_in.at[c, d - 1], outer_send.at[c, d - 1], outer_recv.at[c, d - 1],
                    "yz", q * inner + b,
                )
            )
        outer_copies.append(here)

    for c in range(chunks):
        first(c)
        if c:
            second(c - 1)
    second(chunks - 1)
    for c in range(chunks):
        value = mid[c, a]
        for d in range(1, outer):
            outer_copies[c][d - 1].wait_recv()
            value = value + outer_in[c, d - 1]
        out_ref[:, c * width : (c + 1) * width] = value
    for copy in copies:
        copy.wait_send()
    for c in range(chunks):
        for copy in inner_copies[c] + outer_copies[c]:
            copy.wait_send()


def project(hidden, gain, weight, gx, yz):
    outer, inner = factors(yz)
    rows_each, depth = hidden.shape
    rows = rows_each * gx
    kv, _, columns = weight.shape
    per = 2
    chunks = kv * per
    width = columns // per
    own = rows // yz
    dma = pltpu.SemaphoreType.DMA
    return pl.pallas_call(
        functools.partial(project_kernel, gx, yz, chunks),
        out_shape=jax.ShapeDtypeStruct((own, kv * columns), jnp.float32),
        in_specs=[VMEM, VMEM, VMEM],
        out_specs=VMEM,
        scratch_shapes=[
            pltpu.VMEM((gx, rows_each, depth), jnp.bfloat16),
            pltpu.VMEM((8, rows), jnp.float32),
            pltpu.VMEM((yz - 1, 8, rows), jnp.float32),
            pltpu.VMEM((rows, depth), jnp.bfloat16),
            pltpu.VMEM((chunks, inner, outer, own, width), jnp.float32),
            pltpu.VMEM((chunks, inner - 1, outer, own, width), jnp.float32),
            pltpu.VMEM((chunks, outer, own, width), jnp.float32),
            pltpu.VMEM((chunks, outer - 1, own, width), jnp.float32),
            dma((gx - 1,)), dma((gx - 1,)),
            dma((yz - 1,)), dma((yz - 1,)),
            dma((chunks, inner - 1)), dma((chunks, inner - 1)),
            dma((chunks, outer - 1)), dma((chunks, outer - 1)),
        ],
        compiler_params=pltpu.CompilerParams(
            collective_id=0, has_side_effects=True, vmem_limit_bytes=40 * 2**20
        ),
        name="project",
    )(hidden, gain, weight)


CHUNK = 512


def attend_kernel(
    kv, lengths_ref, proj_ref, cos_ref, sin_ref, key_ref, value_ref, out_ref,
    keys, values, queries, new_keys, new_values, scores, mixed, key_sem, value_sem,
):
    rows = proj_ref.shape[0]
    heads = kv * QUERIES_PER_KEY
    span = CHUNK * kv

    def count(r):
        return (lengths_ref[r] + CHUNK - 1) // CHUNK

    def copy_of(source, target, sems, r, c):
        part = pl.ds(pl.multiple_of(c * span, span), span)
        return pltpu.make_async_copy(source.at[r, part], target.at[r, part], sems.at[r, c])

    def begin(r, _):
        def each(c, _):
            copy_of(key_ref, keys, key_sem, r, c).start()
            copy_of(value_ref, values, value_sem, r, c).start()
            return 0

        return lax.fori_loop(0, count(r), each, 0)

    lax.fori_loop(0, rows, begin, 0)

    cosine, sine = cos_ref[...], sin_ref[...]
    for k in range(kv):
        for s in range(SLOTS):
            at = (k * SLOTS + s) * HEAD_SIZE
            x = proj_ref[:, at : at + HEAD_SIZE]
            if s <= QUERIES_PER_KEY:
                x = x * cosine + pltpu.roll(x, HEAD_SIZE // 2, 1) * sine
            x = x.astype(jnp.bfloat16).astype(jnp.float32)
            if s < QUERIES_PER_KEY:
                queries[:, k * QUERIES_PER_KEY + s, :] = x
            else:
                target = new_keys if s == QUERIES_PER_KEY else new_values
                for h in range(QUERIES_PER_KEY):
                    target[:, k * QUERIES_PER_KEY + h, :] = x

    factor = HEAD_SIZE ** (-0.5)
    column = lax.broadcasted_iota(jnp.int32, (heads, span), 1)
    head = lax.broadcasted_iota(jnp.int32, (heads, span), 0) // QUERIES_PER_KEY
    slot = column // kv
    slot = jnp.where(column - slot * kv == head, slot, 2**30)

    def row(r, _):
        length = lengths_ref[r]
        n = count(r)
        q32 = queries[r]
        q = q32.astype(jnp.bfloat16)
        own = jnp.sum(q32 * new_keys[r], axis=1, keepdims=True) * factor

        def score(c, largest):
            copy_of(key_ref, keys, key_sem, r, c).wait()
            part = pl.ds(pl.multiple_of(c * span, span), span)
            s = lax.dot_general(
                q, keys[r, part, :], (((1,), (1,)), ((), ())), preferred_element_type=jnp.float32
            ) * factor
            s = jnp.where(slot < length - c * CHUNK, s, -jnp.inf)
            scores[c] = s
            return jnp.maximum(largest, jnp.max(s, axis=1, keepdims=True))

        largest = lax.fori_loop(0, n, score, own)

        def weigh(c, total):
            w = jnp.exp(scores[c] - largest)
            scores[c] = w
            return total + jnp.sum(w, axis=1, keepdims=True)

        own_weight = jnp.exp(own - largest)
        total = lax.fori_loop(0, n, weigh, jnp.zeros((heads, 1), jnp.float32)) + own_weight

        def mix(c, acc):
            copy_of(value_ref, values, value_sem, r, c).wait()
            part = pl.ds(pl.multiple_of(c * span, span), span)
            probs = (scores[c] / total).astype(jnp.bfloat16)
            return acc + jnp.dot(probs, values[r, part, :], preferred_element_type=jnp.float32)

        acc = lax.fori_loop(0, n, mix, jnp.zeros((heads, HEAD_SIZE), jnp.float32))
        own_prob = (own_weight / total).astype(jnp.bfloat16).astype(jnp.float32)
        mixed[r] = acc + own_prob * new_values[r]
        return 0

    lax.fori_loop(0, rows, row, 0)
    for h in range(heads):
        out_ref[:, h * HEAD_SIZE : (h + 1) * HEAD_SIZE] = mixed[:, h, :].astype(jnp.bfloat16)


def attend(lengths, proj, cosine, sine, keys, values, kv):
    rows, flat, _ = keys.shape
    heads = kv * QUERIES_PER_KEY
    chunks = flat // kv // CHUNK
    return pl.pallas_call(
        functools.partial(attend_kernel, kv),
        out_shape=jax.ShapeDtypeStruct((rows, heads * HEAD_SIZE), jnp.bfloat16),
        in_specs=[pl.BlockSpec(memory_space=pltpu.SMEM), VMEM, VMEM, VMEM, ANY, ANY],
        out_specs=VMEM,
        scratch_shapes=[
            pltpu.VMEM((rows, flat, HEAD_SIZE), jnp.bfloat16),
            pltpu.VMEM((rows, flat, HEAD_SIZE), jnp.bfloat16),
            pltpu.VMEM((rows, heads, HEAD_SIZE), jnp.float32),
            pltpu.VMEM((rows, heads, HEAD_SIZE), jnp.float32),
            pltpu.VMEM((rows, heads, HEAD_SIZE), jnp.float32),
            pltpu.VMEM((chunks, heads, CHUNK * kv), jnp.float32),
            pltpu.VMEM((rows, heads, HEAD_SIZE), jnp.float32),
            pltpu.SemaphoreType.DMA((rows, chunks)),
            pltpu.SemaphoreType.DMA((rows, chunks)),
        ],
        compiler_params=pltpu.CompilerParams(vmem_limit_bytes=44 * 2**20),
        name="attend",
    )(lengths, proj, cosine, sine, keys, values)


def output_kernel(
    gx, yz, chunks, heads_ref, weight_ref, out_ref,
    gathered, partial, partial_in,
    outer_send, outer_recv, inner_send, inner_recv, sum_send, sum_recv,
):
    outer, inner = factors(yz)
    g = lax.axis_index("gx")
    i = lax.axis_index("yz")
    a = i // inner
    b = lax.rem(i, inner)
    own_rows, depth = heads_ref.shape
    rows = own_rows * yz
    greet(
        [("gx", lax.rem(g + d, gx)) for d in range(1, gx)]
        + [("yz", lax.rem(a + d, outer) * inner + b) for d in range(1, outer)]
        + [("yz", a * inner + lax.rem(b + d, inner)) for d in range(1, inner)]
    )
    outer_copies, inner_copies = [], []
    for d in range(1, outer):
        outer_copies.append(
            start_copy(
                heads_ref, gathered.at[a, b], outer_send.at[d - 1], outer_recv.at[d - 1],
                "yz", lax.rem(a + d, outer) * inner + b,
            )
        )

    def relay(source, q, e):
        for d in range(1, inner):
            inner_copies.append(
                start_copy(
                    source, gathered.at[q, b], inner_send.at[e, d - 1], inner_recv.at[e, d - 1],
                    "yz", a * inner + lax.rem(b + d, inner),
                )
            )

    relay(heads_ref, a, 0)
    gathered[a, b] = heads_ref[...]
    for d in range(1, outer):
        outer_copies[d - 1].wait_recv()
        q = lax.rem(a + outer - d, outer)
        relay(gathered.at[q, b], q, d)
    for copy in inner_copies:
        copy.wait_recv()

    width = out_ref.shape[1] // chunks
    rows_each = rows // gx
    sums = []
    for c in range(chunks):
        part = jnp.dot(
            gathered[...].reshape(rows, depth),
            weight_ref[:, c * width : (c + 1) * width],
            preferred_element_type=jnp.float32,
        ).astype(jnp.bfloat16)
        for p in range(gx):
            partial[c, p] = part[p * rows_each : (p + 1) * rows_each]
        here = []
        for d in range(1, gx):
            p = lax.rem(g + d, gx)
            here.append(
                start_copy(
                    partial.at[c, p], partial_in.at[c, d - 1], sum_send.at[c, d - 1], sum_recv.at[c, d - 1], "gx", p
                )
            )
        sums.append(here)
    for c in range(chunks):
        value = partial[c, g].astype(jnp.float32)
        for d in range(1, gx):
            sums[c][d - 1].wait_recv()
            value = value + partial_in[c, d - 1].astype(jnp.float32)
        out_ref[:, c * width : (c + 1) * width] = value.astype(jnp.bfloat16)
    for copy in outer_copies + inner_copies:
        copy.wait_send()
    for here in sums:
        for copy in here:
            copy.wait_send()


def output(heads, weight, gx, yz):
    outer, inner = factors(yz)
    own, depth = heads.shape
    rows = own * yz
    columns = weight.shape[1]
    chunks = 3
    width = columns // chunks
    dma = pltpu.SemaphoreType.DMA
    return pl.pallas_call(
        functools.partial(output_kernel, gx, yz, chunks),
        out_shape=jax.ShapeDtypeStruct((rows // gx, columns), jnp.bfloat16),
        in_specs=[VMEM, VMEM],
        out_specs=VMEM,
        scratch_shapes=[
            pltpu.VMEM((outer, inner, own, depth), jnp.bfloat16),
            pltpu.VMEM((chunks, gx, rows // gx, width), jnp.bfloat16),
            pltpu.VMEM((chunks, gx - 1, rows // gx, width), jnp.bfloat16),
            dma((outer - 1,)), dma((outer - 1,)),
            dma((outer, inner - 1)), dma((outer, inner - 1)),
            dma((chunks, gx - 1)), dma((chunks, gx - 1)),
        ],
        compiler_params=pltpu.CompilerParams(
            collective_id=1, has_side_effects=True, vmem_limit_bytes=24 * 2**20
        ),
        name="output",
    )(heads, weight)


def body(
    hidden_in, norm_gain, query_key_value_weight, out_weight, key_cache, cached_value_rows, lengths
):
    gx, yz = lax.axis_size("gx"), lax.axis_size("yz")
    own, cached, kv, size = key_cache.shape
    proj = project(
        hidden_in, norm_gain.reshape(1, -1), jnp.transpose(query_key_value_weight, (1, 0, 2)), gx, yz
    )
    half = size // 2
    frequency = ROPE_BASE ** (-(jnp.arange(half, dtype=jnp.float32) * 2.0) / size)
    angles = lengths.astype(jnp.float32)[:, None] * frequency
    cosine, sine = jnp.cos(angles), jnp.sin(angles)
    heads = attend(
        lengths,
        proj,
        jnp.concatenate([cosine, cosine], axis=1),
        jnp.concatenate([-sine, sine], axis=1),
        key_cache.reshape(own, cached * kv, size),
        cached_value_rows.reshape(own, cached * kv, size),
        kv,
    )
    return output(heads, out_weight, gx, yz)


def solution(mesh):
    in_specs = (
        P("gx", "yz"),
        P("yz"),
        P("yz", "gx", None),
        P("gx", "yz"),
        P("yz", None, "gx", None),
        P("yz", None, "gx", None),
        P("yz"),
    )
    out_specs = P("gx", "yz")
    return jax.shard_map(body, mesh=mesh, in_specs=in_specs, out_specs=out_specs, check_vma=False)
```

```python
import functools

import jax
import jax.numpy as jnp
from jax import lax
from jax.experimental import pallas as pl
from jax.experimental.pallas import tpu as pltpu
from jax.sharding import PartitionSpec as P

HEAD_SIZE = 128
QUERIES_PER_KEY = 12
SLOTS = QUERIES_PER_KEY + 2

EPS = 1e-05
ROPE_BASE = 1000000.0
MESH = pl.DeviceIdType.MESH
VMEM = pl.BlockSpec(memory_space=pltpu.VMEM)
ANY = pl.BlockSpec(memory_space=pl.ANY)


def factors(n):
    inner = 1 << ((n.bit_length() - 1) // 2)
    return n // inner, inner


def greet(peers):
    barrier = pltpu.get_barrier_semaphore()
    for axis, index in peers:
        pl.semaphore_signal(barrier, inc=1, device_id={axis: index}, device_id_type=MESH)
    pl.semaphore_wait(barrier, len(peers))


def start_copy(src, dst, send_sem, recv_sem, axis, index):
    copy = pltpu.make_async_remote_copy(
        src_ref=src,
        dst_ref=dst,
        send_sem=send_sem,
        recv_sem=recv_sem,
        device_id={axis: index},
        device_id_type=MESH,
    )
    copy.start()
    return copy


def project_kernel(
    gx, yz, chunks,
    hidden_ref, gain_ref, weight_ref, out_ref,
    hid, squares, squares_in, normed, partial, inner_in, mid, outer_in,
    hid_send, hid_recv, sq_send, sq_recv, inner_send, inner_recv, outer_send, outer_recv,
):
    outer, inner = factors(yz)
    g = lax.axis_index("gx")
    i = lax.axis_index("yz")
    a = i // inner
    b = lax.rem(i, inner)
    greet(
        [("gx", lax.rem(g + d, gx)) for d in range(1, gx)]
        + [("yz", lax.rem(i + d, yz)) for d in range(1, yz)]
    )
    copies = []
    for d in range(1, gx):
        copies.append(
            start_copy(hidden_ref, hid.at[g], hid_send.at[d - 1], hid_recv.at[d - 1], "gx", lax.rem(g + d, gx))
        )
    hid[g] = hidden_ref[...]
    for copy in copies:
        copy.wait_recv()
    rows_each, depth = hidden_ref.shape
    rows = rows_each * gx
    x = hid[...].reshape(rows, depth).astype(jnp.float32)
    own = jnp.sum(x * x, axis=1, keepdims=True)
    squares[...] = jnp.broadcast_to(own, (rows, 128)).T[:8]
    sq_copies = []
    for d in range(1, yz):
        sq_copies.append(
            start_copy(squares, squares_in.at[d - 1], sq_send.at[d - 1], sq_recv.at[d - 1], "yz", lax.rem(i + d, yz))
        )
    total = squares[...]
    for d in range(1, yz):
        sq_copies[d - 1].wait_recv()
        total = total + squares_in[d - 1]
    column = jnp.broadcast_to(total[:1], (128, rows)).T[:, :1]
    scale = lax.rsqrt(column / (depth * yz) + EPS)
    normed[...] = (x * scale * gain_ref[...]).astype(jnp.bfloat16)
    copies += sq_copies

    kv = weight_ref.shape[0]
    per = chunks // kv
    width = weight_ref.shape[2] // per
    own_rows = rows // yz
    inner_copies, outer_copies = [], []

    def first(c):
        part = jnp.dot(
            normed[...],
            weight_ref[c // per, :, (c % per) * width : (c % per + 1) * width],
            preferred_element_type=jnp.float32,
        )
        for q in range(outer):
            for p in range(inner):
                start = (q * inner + p) * own_rows
                partial[c, p, q] = part[start : start + own_rows]
        here = []
        for d in range(1, inner):
            p = lax.rem(b + d, inner)
            here.append(
                start_copy(
                    partial.at[c, p], inner_in.at[c, d - 1], inner_send.at[c, d - 1], inner_recv.at[c, d - 1],
                    "yz", a * inner + p,
                )
            )
        inner_copies.append(here)

    def second(c):
        value = partial[c, b]
        for d in range(1, inner):
            inner_copies[c][d - 1].wait_recv()
            value = value + inner_in[c, d - 1]
        mid[c] = value
        here = []
        for d in range(1, outer):
            q = lax.rem(a + d, outer)
            here.append(
                start_copy(
                    mid.at[c, q], outer_in.at[c, d - 1], outer_send.at[c, d - 1], outer_recv.at[c, d - 1],
                    "yz", q * inner + b,
                )
            )
        outer_copies.append(here)

    for c in range(chunks):
        first(c)
        if c:
            second(c - 1)
    second(chunks - 1)
    for c in range(chunks):
        value = mid[c, a]
        for d in range(1, outer):
            outer_copies[c][d - 1].wait_recv()
            value = value + outer_in[c, d - 1]
        out_ref[:, c * width : (c + 1) * width] = value
    for copy in copies:
        copy.wait_send()
    for c in range(chunks):
        for copy in inner_copies[c] + outer_copies[c]:
            copy.wait_send()


def project(hidden, gain, weight, gx, yz):
    outer, inner = factors(yz)
    rows_each, depth = hidden.shape
    rows = rows_each * gx
    kv, _, columns = weight.shape
    per = columns // 256
    chunks = kv * per
    width = columns // per
    own = rows // yz
    dma = pltpu.SemaphoreType.DMA
    return pl.pallas_call(
        functools.partial(project_kernel, gx, yz, chunks),
        out_shape=jax.ShapeDtypeStruct((own, kv * columns), jnp.float32),
        in_specs=[VMEM, VMEM, VMEM],
        out_specs=VMEM,
        scratch_shapes=[
            pltpu.VMEM((gx, rows_each, depth), jnp.bfloat16),
            pltpu.VMEM((8, rows), jnp.float32),
            pltpu.VMEM((yz - 1, 8, rows), jnp.float32),
            pltpu.VMEM((rows, depth), jnp.bfloat16),
            pltpu.VMEM((chunks, inner, outer, own, width), jnp.float32),
            pltpu.VMEM((chunks, inner - 1, outer, own, width), jnp.float32),
            pltpu.VMEM((chunks, outer, own, width), jnp.float32),
            pltpu.VMEM((chunks, outer - 1, own, width), jnp.float32),
            dma((gx - 1,)), dma((gx - 1,)),
            dma((yz - 1,)), dma((yz - 1,)),
            dma((chunks, inner - 1)), dma((chunks, inner - 1)),
            dma((chunks, outer - 1)), dma((chunks, outer - 1)),
        ],
        compiler_params=pltpu.CompilerParams(
            collective_id=0, has_side_effects=True, vmem_limit_bytes=10 * 2**20
        ),
        name="project",
    )(hidden, gain, weight)


CHUNK = 512


def attend_kernel(
    kv, lengths_ref, proj_ref, cos_ref, sin_ref, key_ref, value_ref, out_ref,
    values, queries, new_keys, new_values, scores, mixed, value_sem,
):
    rows = proj_ref.shape[0]
    heads = kv * QUERIES_PER_KEY
    span = CHUNK * kv

    def count(r):
        first = r // 2 * 2
        longer = jnp.maximum(lengths_ref[first], lengths_ref[first + 1])
        return (longer + CHUNK - 1) // CHUNK

    def copy_of(r, c):
        part = pl.ds(pl.multiple_of(c * span, span), span)
        return pltpu.make_async_copy(value_ref.at[r, part], values.at[r, part], value_sem.at[r, c])

    def begin(r, _):
        def each(c, _):
            copy_of(r, c).start()
            return 0

        return lax.fori_loop(0, count(r), each, 0)

    lax.fori_loop(0, rows, begin, 0)

    cosine, sine = cos_ref[...], sin_ref[...]
    for k in range(kv):
        for s in range(SLOTS):
            at = (k * SLOTS + s) * HEAD_SIZE
            x = proj_ref[:, at : at + HEAD_SIZE]
            if s <= QUERIES_PER_KEY:
                x = x * cosine + pltpu.roll(x, HEAD_SIZE // 2, 1) * sine
            x = x.astype(jnp.bfloat16).astype(jnp.float32)
            if s < QUERIES_PER_KEY:
                queries[:, k * QUERIES_PER_KEY + s, :] = x
            else:
                target = new_keys if s == QUERIES_PER_KEY else new_values
                for h in range(QUERIES_PER_KEY):
                    target[:, k * QUERIES_PER_KEY + h, :] = x

    factor = HEAD_SIZE ** (-0.5)
    column = lax.broadcasted_iota(jnp.int32, (heads, span), 1)
    head = lax.broadcasted_iota(jnp.int32, (heads, span), 0) // QUERIES_PER_KEY
    slot = column // kv
    slot = jnp.where(column - slot * kv == head, slot, 2**30)

    def pair(r, n):
        both = (0, 1)
        q32 = [queries[r + e] for e in both]
        lengths = [lengths_ref[r + e] for e in both]
        own = [jnp.sum(q32[e] * new_keys[r + e], axis=1, keepdims=True) * factor for e in both]
        largest = [None, None]
        for c in range(n):
            for e in both:
                s = lax.dot_general(
                    q32[e].astype(jnp.bfloat16),
                    key_ref[r + e, c * span : (c + 1) * span, :],
                    (((1,), (1,)), ((), ())),
                    preferred_element_type=jnp.float32,
                ) * factor
                s = jnp.where(slot < lengths[e] - c * CHUNK, s, -jnp.inf)
                scores[e, c] = s
                best = functools.reduce(
                    jnp.maximum, [s[:, t : t + 128] for t in range(0, span, 128)]
                )
                largest[e] = best if c == 0 else jnp.maximum(largest[e], best)
        largest = [
            jnp.maximum(jnp.max(largest[e], axis=1, keepdims=True), own[e]) for e in both
        ]
        own_weight = [jnp.exp(own[e] - largest[e]) for e in both]
        total = [None, None]
        for c in range(n):
            for e in both:
                w = jnp.exp(scores[e, c] - largest[e])
                scores[e, c] = w
                add = functools.reduce(
                    lambda x, y: x + y, [w[:, t : t + 128] for t in range(0, span, 128)]
                )
                total[e] = add if c == 0 else total[e] + add
        total = [jnp.sum(total[e], axis=1, keepdims=True) + own_weight[e] for e in both]
        inverse = [1.0 / total[e] for e in both]
        for c in range(n):
            for e in both:
                copy_of(r + e, c).wait()
        for e in both:
            acc = jnp.zeros((heads, HEAD_SIZE), jnp.float32)
            for c in range(n):
                probs = (scores[e, c] * inverse[e]).astype(jnp.bfloat16)
                acc = acc + jnp.dot(
                    probs,
                    values[r + e, c * span : (c + 1) * span, :],
                    preferred_element_type=jnp.float32,
                )
            own_prob = (own_weight[e] * inverse[e]).astype(jnp.bfloat16).astype(jnp.float32)
            mixed[r + e] = acc + own_prob * new_values[r + e]

    def step(p, _):
        r = p * 2
        needed = count(r)
        for n in range(1, scores.shape[1] + 1):
            pl.when(needed == n)(functools.partial(pair, r, n))
        return 0

    lax.fori_loop(0, rows // 2, step, 0)
    for h in range(heads):
        out_ref[:, h * HEAD_SIZE : (h + 1) * HEAD_SIZE] = mixed[:, h, :].astype(jnp.bfloat16)


def attend(lengths, proj, cosine, sine, keys, values, kv):
    rows, flat, _ = keys.shape
    heads = kv * QUERIES_PER_KEY
    chunks = flat // kv // CHUNK
    return pl.pallas_call(
        functools.partial(attend_kernel, kv),
        out_shape=jax.ShapeDtypeStruct((rows, heads * HEAD_SIZE), jnp.bfloat16),
        in_specs=[pl.BlockSpec(memory_space=pltpu.SMEM), VMEM, VMEM, VMEM, VMEM, ANY],
        out_specs=VMEM,
        scratch_shapes=[
            pltpu.VMEM((rows, flat, HEAD_SIZE), jnp.bfloat16),
            pltpu.VMEM((rows, heads, HEAD_SIZE), jnp.float32),
            pltpu.VMEM((rows, heads, HEAD_SIZE), jnp.float32),
            pltpu.VMEM((rows, heads, HEAD_SIZE), jnp.float32),
            pltpu.VMEM((2, chunks, heads, CHUNK * kv), jnp.float32),
            pltpu.VMEM((rows, heads, HEAD_SIZE), jnp.float32),
            pltpu.SemaphoreType.DMA((rows, chunks)),
        ],
        compiler_params=pltpu.CompilerParams(vmem_limit_bytes=22 * 2**20),
        name="attend",
    )(lengths, proj, cosine, sine, keys, values)


def output_kernel(
    gx, yz, chunks, heads_ref, weight_ref, out_ref,
    gathered, partial, partial_in,
    outer_send, outer_recv, inner_send, inner_recv, sum_send, sum_recv,
):
    outer, inner = factors(yz)
    g = lax.axis_index("gx")
    i = lax.axis_index("yz")
    a = i // inner
    b = lax.rem(i, inner)
    own_rows, depth = heads_ref.shape
    rows = own_rows * yz
    greet(
        [("gx", lax.rem(g + d, gx)) for d in range(1, gx)]
        + [("yz", lax.rem(a + d, outer) * inner + b) for d in range(1, outer)]
        + [("yz", a * inner + lax.rem(b + d, inner)) for d in range(1, inner)]
    )
    outer_copies, inner_copies = [], []
    for d in range(1, outer):
        outer_copies.append(
            start_copy(
                heads_ref, gathered.at[a, b], outer_send.at[d - 1], outer_recv.at[d - 1],
                "yz", lax.rem(a + d, outer) * inner + b,
            )
        )

    def relay(source, q, e):
        for d in range(1, inner):
            inner_copies.append(
                start_copy(
                    source, gathered.at[q, b], inner_send.at[e, d - 1], inner_recv.at[e, d - 1],
                    "yz", a * inner + lax.rem(b + d, inner),
                )
            )

    relay(heads_ref, a, 0)
    gathered[a, b] = heads_ref[...]
    for d in range(1, outer):
        outer_copies[d - 1].wait_recv()
        q = lax.rem(a + outer - d, outer)
        relay(gathered.at[q, b], q, d)
    for copy in inner_copies:
        copy.wait_recv()

    width = out_ref.shape[1] // chunks
    rows_each = rows // gx
    sums = []
    for c in range(chunks):
        part = jnp.dot(
            gathered[...].reshape(rows, depth),
            weight_ref[:, c * width : (c + 1) * width],
            preferred_element_type=jnp.float32,
        ).astype(jnp.bfloat16)
        for p in range(gx):
            partial[c, p] = part[p * rows_each : (p + 1) * rows_each]
        here = []
        for d in range(1, gx):
            p = lax.rem(g + d, gx)
            here.append(
                start_copy(
                    partial.at[c, p], partial_in.at[c, d - 1], sum_send.at[c, d - 1], sum_recv.at[c, d - 1], "gx", p
                )
            )
        sums.append(here)
    for c in range(chunks):
        value = partial[c, g].astype(jnp.float32)
        for d in range(1, gx):
            sums[c][d - 1].wait_recv()
            value = value + partial_in[c, d - 1].astype(jnp.float32)
        out_ref[:, c * width : (c + 1) * width] = value.astype(jnp.bfloat16)
    for copy in outer_copies + inner_copies:
        copy.wait_send()
    for here in sums:
        for copy in here:
            copy.wait_send()


def output(heads, weight, gx, yz):
    outer, inner = factors(yz)
    own, depth = heads.shape
    rows = own * yz
    columns = weight.shape[1]
    chunks = 3
    width = columns // chunks
    dma = pltpu.SemaphoreType.DMA
    return pl.pallas_call(
        functools.partial(output_kernel, gx, yz, chunks),
        out_shape=jax.ShapeDtypeStruct((rows // gx, columns), jnp.bfloat16),
        in_specs=[VMEM, VMEM],
        out_specs=VMEM,
        scratch_shapes=[
            pltpu.VMEM((outer, inner, own, depth), jnp.bfloat16),
            pltpu.VMEM((chunks, gx, rows // gx, width), jnp.bfloat16),
            pltpu.VMEM((chunks, gx - 1, rows // gx, width), jnp.bfloat16),
            dma((outer - 1,)), dma((outer - 1,)),
            dma((outer, inner - 1)), dma((outer, inner - 1)),
            dma((chunks, gx - 1)), dma((chunks, gx - 1)),
        ],
        compiler_params=pltpu.CompilerParams(
            collective_id=1, has_side_effects=True, vmem_limit_bytes=6 * 2**20
        ),
        name="output",
    )(heads, weight)


def body(
    hidden_in, norm_gain, query_key_value_weight, out_weight, key_cache, cached_value_rows, lengths
):
    gx, yz = lax.axis_size("gx"), lax.axis_size("yz")
    own, cached, kv, size = key_cache.shape
    proj = project(
        hidden_in, norm_gain.reshape(1, -1), jnp.transpose(query_key_value_weight, (1, 0, 2)), gx, yz
    )
    half = size // 2
    frequency = ROPE_BASE ** (-(jnp.arange(half, dtype=jnp.float32) * 2.0) / size)
    angles = lengths.astype(jnp.float32)[:, None] * frequency
    cosine, sine = jnp.cos(angles), jnp.sin(angles)
    heads = attend(
        lengths,
        proj,
        jnp.concatenate([cosine, cosine], axis=1),
        jnp.concatenate([-sine, sine], axis=1),
        key_cache.reshape(own, cached * kv, size),
        cached_value_rows.reshape(own, cached * kv, size),
        kv,
    )
    return output(heads, out_weight, gx, yz)


def solution(mesh):
    in_specs = (
        P("gx", "yz"),
        P("yz"),
        P("yz", "gx", None),
        P("gx", "yz"),
        P("yz", None, "gx", None),
        P("yz", None, "gx", None),
        P("yz"),
    )
    out_specs = P("gx", "yz")
    return jax.shard_map(body, mesh=mesh, in_specs=in_specs, out_specs=out_specs, check_vma=False)
```

```python
import functools

import jax
import jax.numpy as jnp
from jax import lax
from jax.experimental import pallas as pl
from jax.experimental.pallas import tpu as pltpu
from jax.sharding import PartitionSpec as P

HEAD_SIZE = 128
QUERIES_PER_KEY = 12
SLOTS = QUERIES_PER_KEY + 2

EPS = 1e-05
ROPE_BASE = 1000000.0
MESH = pl.DeviceIdType.MESH
VMEM = pl.BlockSpec(memory_space=pltpu.VMEM)
ANY = pl.BlockSpec(memory_space=pl.ANY)


def factors(n):
    inner = 1 << ((n.bit_length() - 1) // 2)
    return n // inner, inner


def greet(peers):
    barrier = pltpu.get_barrier_semaphore()
    for axis, index in peers:
        pl.semaphore_signal(barrier, inc=1, device_id={axis: index}, device_id_type=MESH)
    pl.semaphore_wait(barrier, len(peers))


def start_copy(src, dst, send_sem, recv_sem, axis, index):
    copy = pltpu.make_async_remote_copy(
        src_ref=src,
        dst_ref=dst,
        send_sem=send_sem,
        recv_sem=recv_sem,
        device_id={axis: index},
        device_id_type=MESH,
    )
    copy.start()
    return copy


def project_kernel(
    gx, yz, chunks,
    hidden_ref, gain_ref, weight_ref, out_ref,
    hid, squares, squares_in, normed, partial, inner_in, mid, outer_in,
    hid_send, hid_recv, sq_send, sq_recv, inner_send, inner_recv, outer_send, outer_recv,
):
    outer, inner = factors(yz)
    g = lax.axis_index("gx")
    i = lax.axis_index("yz")
    a = i // inner
    b = lax.rem(i, inner)
    greet(
        [("gx", lax.rem(g + d, gx)) for d in range(1, gx)]
        + [("yz", lax.rem(i + d, yz)) for d in range(1, yz)]
    )
    copies = []
    for d in range(1, gx):
        copies.append(
            start_copy(hidden_ref, hid.at[g], hid_send.at[d - 1], hid_recv.at[d - 1], "gx", lax.rem(g + d, gx))
        )
    hid[g] = hidden_ref[...]
    for copy in copies:
        copy.wait_recv()
    rows_each, depth = hidden_ref.shape
    rows = rows_each * gx
    x = hid[...].reshape(rows, depth).astype(jnp.float32)
    own = jnp.sum(x * x, axis=1, keepdims=True)
    squares[...] = jnp.broadcast_to(own, (rows, 128)).T[:8]
    sq_copies = []
    for d in range(1, yz):
        sq_copies.append(
            start_copy(squares, squares_in.at[d - 1], sq_send.at[d - 1], sq_recv.at[d - 1], "yz", lax.rem(i + d, yz))
        )
    total = squares[...]
    for d in range(1, yz):
        sq_copies[d - 1].wait_recv()
        total = total + squares_in[d - 1]
    column = jnp.broadcast_to(total[:1], (128, rows)).T[:, :1]
    scale = lax.rsqrt(column / (depth * yz) + EPS)
    normed[...] = (x * scale * gain_ref[...]).astype(jnp.bfloat16)
    copies += sq_copies

    kv = weight_ref.shape[0]
    per = chunks // kv
    width = weight_ref.shape[2] // per
    own_rows = rows // yz
    inner_copies, outer_copies = [], []

    def first(c):
        part = jnp.dot(
            normed[...],
            weight_ref[c // per, :, (c % per) * width : (c % per + 1) * width],
            preferred_element_type=jnp.float32,
        )
        for q in range(outer):
            for p in range(inner):
                start = (q * inner + p) * own_rows
                partial[c, p, q] = part[start : start + own_rows]
        here = []
        for d in range(1, inner):
            p = lax.rem(b + d, inner)
            here.append(
                start_copy(
                    partial.at[c, p], inner_in.at[c, d - 1], inner_send.at[c, d - 1], inner_recv.at[c, d - 1],
                    "yz", a * inner + p,
                )
            )
        inner_copies.append(here)

    def second(c):
        value = partial[c, b]
        for d in range(1, inner):
            inner_copies[c][d - 1].wait_recv()
            value = value + inner_in[c, d - 1]
        mid[c] = value
        here = []
        for d in range(1, outer):
            q = lax.rem(a + d, outer)
            here.append(
                start_copy(
                    mid.at[c, q], outer_in.at[c, d - 1], outer_send.at[c, d - 1], outer_recv.at[c, d - 1],
                    "yz", q * inner + b,
                )
            )
        outer_copies.append(here)

    for c in range(chunks):
        first(c)
        if c:
            second(c - 1)
    second(chunks - 1)
    for c in range(chunks):
        value = mid[c, a]
        for d in range(1, outer):
            outer_copies[c][d - 1].wait_recv()
            value = value + outer_in[c, d - 1]
        out_ref[:, c * width : (c + 1) * width] = value
    for copy in copies:
        copy.wait_send()
    for c in range(chunks):
        for copy in inner_copies[c] + outer_copies[c]:
            copy.wait_send()


def project(hidden, gain, weight, gx, yz):
    outer, inner = factors(yz)
    rows_each, depth = hidden.shape
    rows = rows_each * gx
    kv, _, columns = weight.shape
    per = 2
    chunks = kv * per
    width = columns // per
    own = rows // yz
    dma = pltpu.SemaphoreType.DMA
    return pl.pallas_call(
        functools.partial(project_kernel, gx, yz, chunks),
        out_shape=jax.ShapeDtypeStruct((own, kv * columns), jnp.float32),
        in_specs=[VMEM, VMEM, VMEM],
        out_specs=VMEM,
        scratch_shapes=[
            pltpu.VMEM((gx, rows_each, depth), jnp.bfloat16),
            pltpu.VMEM((8, rows), jnp.float32),
            pltpu.VMEM((yz - 1, 8, rows), jnp.float32),
            pltpu.VMEM((rows, depth), jnp.bfloat16),
            pltpu.VMEM((chunks, inner, outer, own, width), jnp.float32),
            pltpu.VMEM((chunks, inner - 1, outer, own, width), jnp.float32),
            pltpu.VMEM((chunks, outer, own, width), jnp.float32),
            pltpu.VMEM((chunks, outer - 1, own, width), jnp.float32),
            dma((gx - 1,)), dma((gx - 1,)),
            dma((yz - 1,)), dma((yz - 1,)),
            dma((chunks, inner - 1)), dma((chunks, inner - 1)),
            dma((chunks, outer - 1)), dma((chunks, outer - 1)),
        ],
        compiler_params=pltpu.CompilerParams(
            collective_id=0, has_side_effects=True, vmem_limit_bytes=10 * 2**20
        ),
        name="project",
    )(hidden, gain, weight)


CHUNK = 512


def attend_kernel(
    kv, lengths_ref, proj_ref, cos_ref, sin_ref, key_ref, value_ref, out_ref,
    values, queries, new_keys, new_values, scores, mixed, value_sem,
):
    rows = proj_ref.shape[0]
    heads = kv * QUERIES_PER_KEY
    span = CHUNK * kv

    def count(r):
        first = r // 2 * 2
        longer = jnp.maximum(lengths_ref[first], lengths_ref[first + 1])
        return (longer + CHUNK - 1) // CHUNK

    def copy_of(r, c):
        part = pl.ds(pl.multiple_of(c * span, span), span)
        return pltpu.make_async_copy(value_ref.at[r, part], values.at[r, part], value_sem.at[r, c])

    def begin(r, _):
        def each(c, _):
            copy_of(r, c).start()
            return 0

        return lax.fori_loop(0, count(r), each, 0)

    lax.fori_loop(0, rows, begin, 0)

    cosine, sine = cos_ref[...], sin_ref[...]
    for k in range(kv):
        for s in range(SLOTS):
            at = (k * SLOTS + s) * HEAD_SIZE
            x = proj_ref[:, at : at + HEAD_SIZE]
            if s <= QUERIES_PER_KEY:
                x = x * cosine + pltpu.roll(x, HEAD_SIZE // 2, 1) * sine
            x = x.astype(jnp.bfloat16).astype(jnp.float32)
            if s < QUERIES_PER_KEY:
                queries[:, k * QUERIES_PER_KEY + s, :] = x
            else:
                target = new_keys if s == QUERIES_PER_KEY else new_values
                for h in range(QUERIES_PER_KEY):
                    target[:, k * QUERIES_PER_KEY + h, :] = x

    factor = HEAD_SIZE ** (-0.5)
    column = lax.broadcasted_iota(jnp.int32, (heads, span), 1)
    head = lax.broadcasted_iota(jnp.int32, (heads, span), 0) // QUERIES_PER_KEY
    slot = column // kv
    slot = jnp.where(column - slot * kv == head, slot, 2**30)

    def pair(r, n):
        both = (0, 1)
        q32 = [queries[r + e] for e in both]
        lengths = [lengths_ref[r + e] for e in both]
        own = [jnp.sum(q32[e] * new_keys[r + e], axis=1, keepdims=True) * factor for e in both]
        largest = [None, None]
        for c in range(n):
            for e in both:
                s = lax.dot_general(
                    q32[e].astype(jnp.bfloat16),
                    key_ref[r + e, c * span : (c + 1) * span, :],
                    (((1,), (1,)), ((), ())),
                    preferred_element_type=jnp.float32,
                ) * factor
                s = jnp.where(slot < lengths[e] - c * CHUNK, s, -jnp.inf)
                scores[e, c] = s
                best = functools.reduce(
                    jnp.maximum, [s[:, t : t + 128] for t in range(0, span, 128)]
                )
                largest[e] = best if c == 0 else jnp.maximum(largest[e], best)
        largest = [
            jnp.maximum(jnp.max(largest[e], axis=1, keepdims=True), own[e]) for e in both
        ]
        own_weight = [jnp.exp(own[e] - largest[e]) for e in both]
        total = [None, None]
        for c in range(n):
            for e in both:
                w = jnp.exp(scores[e, c] - largest[e])
                scores[e, c] = w
                add = functools.reduce(
                    lambda x, y: x + y, [w[:, t : t + 128] for t in range(0, span, 128)]
                )
                total[e] = add if c == 0 else total[e] + add
        total = [jnp.sum(total[e], axis=1, keepdims=True) + own_weight[e] for e in both]
        inverse = [1.0 / total[e] for e in both]
        for c in range(n):
            for e in both:
                copy_of(r + e, c).wait()
        for e in both:
            acc = jnp.zeros((heads, HEAD_SIZE), jnp.float32)
            for c in range(n):
                probs = (scores[e, c] * inverse[e]).astype(jnp.bfloat16)
                acc = acc + jnp.dot(
                    probs,
                    values[r + e, c * span : (c + 1) * span, :],
                    preferred_element_type=jnp.float32,
                )
            own_prob = (own_weight[e] * inverse[e]).astype(jnp.bfloat16).astype(jnp.float32)
            mixed[r + e] = acc + own_prob * new_values[r + e]

    def step(p, _):
        r = p * 2
        needed = count(r)
        for n in range(1, scores.shape[1] + 1):
            pl.when(needed == n)(functools.partial(pair, r, n))
        return 0

    lax.fori_loop(0, rows // 2, step, 0)
    for h in range(heads):
        out_ref[:, h * HEAD_SIZE : (h + 1) * HEAD_SIZE] = mixed[:, h, :].astype(jnp.bfloat16)


def attend(lengths, proj, cosine, sine, keys, values, kv):
    rows, flat, _ = keys.shape
    heads = kv * QUERIES_PER_KEY
    chunks = flat // kv // CHUNK
    return pl.pallas_call(
        functools.partial(attend_kernel, kv),
        out_shape=jax.ShapeDtypeStruct((rows, heads * HEAD_SIZE), jnp.bfloat16),
        in_specs=[pl.BlockSpec(memory_space=pltpu.SMEM), VMEM, VMEM, VMEM, VMEM, ANY],
        out_specs=VMEM,
        scratch_shapes=[
            pltpu.VMEM((rows, flat, HEAD_SIZE), jnp.bfloat16),
            pltpu.VMEM((rows, heads, HEAD_SIZE), jnp.float32),
            pltpu.VMEM((rows, heads, HEAD_SIZE), jnp.float32),
            pltpu.VMEM((rows, heads, HEAD_SIZE), jnp.float32),
            pltpu.VMEM((2, chunks, heads, CHUNK * kv), jnp.float32),
            pltpu.VMEM((rows, heads, HEAD_SIZE), jnp.float32),
            pltpu.SemaphoreType.DMA((rows, chunks)),
        ],
        compiler_params=pltpu.CompilerParams(vmem_limit_bytes=22 * 2**20),
        name="attend",
    )(lengths, proj, cosine, sine, keys, values)


def output_kernel(
    gx, yz, chunks, heads_ref, weight_ref, out_ref,
    gathered, partial, partial_in,
    outer_send, outer_recv, inner_send, inner_recv, sum_send, sum_recv,
):
    outer, inner = factors(yz)
    g = lax.axis_index("gx")
    i = lax.axis_index("yz")
    a = i // inner
    b = lax.rem(i, inner)
    own_rows, depth = heads_ref.shape
    rows = own_rows * yz
    greet(
        [("gx", lax.rem(g + d, gx)) for d in range(1, gx)]
        + [("yz", lax.rem(a + d, outer) * inner + b) for d in range(1, outer)]
        + [("yz", a * inner + lax.rem(b + d, inner)) for d in range(1, inner)]
    )
    outer_copies, inner_copies = [], []
    for d in range(1, outer):
        outer_copies.append(
            start_copy(
                heads_ref, gathered.at[a, b], outer_send.at[d - 1], outer_recv.at[d - 1],
                "yz", lax.rem(a + d, outer) * inner + b,
            )
        )

    def relay(source, q, e):
        for d in range(1, inner):
            inner_copies.append(
                start_copy(
                    source, gathered.at[q, b], inner_send.at[e, d - 1], inner_recv.at[e, d - 1],
                    "yz", a * inner + lax.rem(b + d, inner),
                )
            )

    relay(heads_ref, a, 0)
    gathered[a, b] = heads_ref[...]
    for d in range(1, outer):
        outer_copies[d - 1].wait_recv()
        q = lax.rem(a + outer - d, outer)
        relay(gathered.at[q, b], q, d)
    for copy in inner_copies:
        copy.wait_recv()

    width = out_ref.shape[1] // chunks
    rows_each = rows // gx
    sums = []
    for c in range(chunks):
        part = jnp.dot(
            gathered[...].reshape(rows, depth),
            weight_ref[:, c * width : (c + 1) * width],
            preferred_element_type=jnp.float32,
        ).astype(jnp.bfloat16)
        for p in range(gx):
            partial[c, p] = part[p * rows_each : (p + 1) * rows_each]
        here = []
        for d in range(1, gx):
            p = lax.rem(g + d, gx)
            here.append(
                start_copy(
                    partial.at[c, p], partial_in.at[c, d - 1], sum_send.at[c, d - 1], sum_recv.at[c, d - 1], "gx", p
                )
            )
        sums.append(here)
    for c in range(chunks):
        value = partial[c, g].astype(jnp.float32)
        for d in range(1, gx):
            sums[c][d - 1].wait_recv()
            value = value + partial_in[c, d - 1].astype(jnp.float32)
        out_ref[:, c * width : (c + 1) * width] = value.astype(jnp.bfloat16)
    for copy in outer_copies + inner_copies:
        copy.wait_send()
    for here in sums:
        for copy in here:
            copy.wait_send()


def output(heads, weight, gx, yz):
    outer, inner = factors(yz)
    own, depth = heads.shape
    rows = own * yz
    columns = weight.shape[1]
    chunks = 3
    width = columns // chunks
    dma = pltpu.SemaphoreType.DMA
    return pl.pallas_call(
        functools.partial(output_kernel, gx, yz, chunks),
        out_shape=jax.ShapeDtypeStruct((rows // gx, columns), jnp.bfloat16),
        in_specs=[VMEM, VMEM],
        out_specs=VMEM,
        scratch_shapes=[
            pltpu.VMEM((outer, inner, own, depth), jnp.bfloat16),
            pltpu.VMEM((chunks, gx, rows // gx, width), jnp.bfloat16),
            pltpu.VMEM((chunks, gx - 1, rows // gx, width), jnp.bfloat16),
            dma((outer - 1,)), dma((outer - 1,)),
            dma((outer, inner - 1)), dma((outer, inner - 1)),
            dma((chunks, gx - 1)), dma((chunks, gx - 1)),
        ],
        compiler_params=pltpu.CompilerParams(
            collective_id=1, has_side_effects=True, vmem_limit_bytes=6 * 2**20
        ),
        name="output",
    )(heads, weight)


def body(
    hidden_in, norm_gain, query_key_value_weight, out_weight, key_cache, cached_value_rows, lengths
):
    gx, yz = lax.axis_size("gx"), lax.axis_size("yz")
    own, cached, kv, size = key_cache.shape
    proj = project(
        hidden_in, norm_gain.reshape(1, -1), jnp.transpose(query_key_value_weight, (1, 0, 2)), gx, yz
    )
    half = size // 2
    frequency = ROPE_BASE ** (-(jnp.arange(half, dtype=jnp.float32) * 2.0) / size)
    angles = lengths.astype(jnp.float32)[:, None] * frequency
    cosine, sine = jnp.cos(angles), jnp.sin(angles)
    heads = attend(
        lengths,
        proj,
        jnp.concatenate([cosine, cosine], axis=1),
        jnp.concatenate([-sine, sine], axis=1),
        key_cache.reshape(own, cached * kv, size),
        cached_value_rows.reshape(own, cached * kv, size),
        kv,
    )
    return output(heads, out_weight, gx, yz)


def solution(mesh):
    in_specs = (
        P("gx", "yz"),
        P("yz"),
        P("yz", "gx", None),
        P("gx", "yz"),
        P("yz", None, "gx", None),
        P("yz", None, "gx", None),
        P("yz"),
    )
    out_specs = P("gx", "yz")
    return jax.shard_map(body, mesh=mesh, in_specs=in_specs, out_specs=out_specs, check_vma=False)
```

```python
import functools

import jax
import jax.numpy as jnp
from jax import lax
from jax.experimental import pallas as pl
from jax.experimental.pallas import tpu as pltpu
from jax.sharding import PartitionSpec as P

HEAD_SIZE = 128
QUERIES_PER_KEY = 12
SLOTS = QUERIES_PER_KEY + 2

EPS = 1e-05
ROPE_BASE = 1000000.0
MESH = pl.DeviceIdType.MESH
VMEM = pl.BlockSpec(memory_space=pltpu.VMEM)
ANY = pl.BlockSpec(memory_space=pl.ANY)


def factors(n):
    inner = 1 << ((n.bit_length() - 1) // 2)
    return n // inner, inner


def greet(peers):
    barrier = pltpu.get_barrier_semaphore()
    for axis, index in peers:
        pl.semaphore_signal(barrier, inc=1, device_id={axis: index}, device_id_type=MESH)
    pl.semaphore_wait(barrier, len(peers))


def start_copy(src, dst, send_sem, recv_sem, axis, index):
    copy = pltpu.make_async_remote_copy(
        src_ref=src,
        dst_ref=dst,
        send_sem=send_sem,
        recv_sem=recv_sem,
        device_id={axis: index},
        device_id_type=MESH,
    )
    copy.start()
    return copy


def project_kernel(
    gx, yz, chunks,
    hidden_ref, gain_ref, weight_ref, out_ref,
    hid, squares, squares_in, normed, partial, inner_in, mid, outer_in,
    hid_send, hid_recv, sq_send, sq_recv, inner_send, inner_recv, outer_send, outer_recv,
):
    outer, inner = factors(yz)
    g = lax.axis_index("gx")
    i = lax.axis_index("yz")
    a = i // inner
    b = lax.rem(i, inner)
    greet(
        [("gx", lax.rem(g + d, gx)) for d in range(1, gx)]
        + [("yz", lax.rem(i + d, yz)) for d in range(1, yz)]
    )
    copies = []
    for d in range(1, gx):
        copies.append(
            start_copy(hidden_ref, hid.at[g], hid_send.at[d - 1], hid_recv.at[d - 1], "gx", lax.rem(g + d, gx))
        )
    hid[g] = hidden_ref[...]
    for copy in copies:
        copy.wait_recv()
    rows_each, depth = hidden_ref.shape
    rows = rows_each * gx
    x = hid[...].reshape(rows, depth).astype(jnp.float32)
    own = jnp.sum(x * x, axis=1, keepdims=True)
    squares[...] = jnp.broadcast_to(own, (rows, 128)).T[:8]
    sq_copies = []
    for d in range(1, yz):
        sq_copies.append(
            start_copy(squares, squares_in.at[d - 1], sq_send.at[d - 1], sq_recv.at[d - 1], "yz", lax.rem(i + d, yz))
        )
    total = squares[...]
    for d in range(1, yz):
        sq_copies[d - 1].wait_recv()
        total = total + squares_in[d - 1]
    column = jnp.broadcast_to(total[:1], (128, rows)).T[:, :1]
    scale = lax.rsqrt(column / (depth * yz) + EPS)
    normed[...] = (x * scale * gain_ref[...]).astype(jnp.bfloat16)
    copies += sq_copies

    kv = weight_ref.shape[0]
    per = chunks // kv
    width = weight_ref.shape[2] // per
    own_rows = rows // yz
    inner_copies, outer_copies = [], []

    def first(c):
        part = jnp.dot(
            normed[...],
            weight_ref[c // per, :, (c % per) * width : (c % per + 1) * width],
            preferred_element_type=jnp.float32,
        )
        for q in range(outer):
            for p in range(inner):
                start = (q * inner + p) * own_rows
                partial[c, p, q] = part[start : start + own_rows]
        here = []
        for d in range(1, inner):
            p = lax.rem(b + d, inner)
            here.append(
                start_copy(
                    partial.at[c, p], inner_in.at[c, d - 1], inner_send.at[c, d - 1], inner_recv.at[c, d - 1],
                    "yz", a * inner + p,
                )
            )
        inner_copies.append(here)

    def second(c):
        value = partial[c, b]
        for d in range(1, inner):
            inner_copies[c][d - 1].wait_recv()
            value = value + inner_in[c, d - 1]
        mid[c] = value
        here = []
        for d in range(1, outer):
            q = lax.rem(a + d, outer)
            here.append(
                start_copy(
                    mid.at[c, q], outer_in.at[c, d - 1], outer_send.at[c, d - 1], outer_recv.at[c, d - 1],
                    "yz", q * inner + b,
                )
            )
        outer_copies.append(here)

    for c in range(chunks):
        first(c)
        if c:
            second(c - 1)
    second(chunks - 1)
    for c in range(chunks):
        value = mid[c, a]
        for d in range(1, outer):
            outer_copies[c][d - 1].wait_recv()
            value = value + outer_in[c, d - 1]
        out_ref[:, c * width : (c + 1) * width] = value
    for copy in copies:
        copy.wait_send()
    for c in range(chunks):
        for copy in inner_copies[c] + outer_copies[c]:
            copy.wait_send()


def project(hidden, gain, weight, gx, yz):
    outer, inner = factors(yz)
    rows_each, depth = hidden.shape
    rows = rows_each * gx
    kv, _, columns = weight.shape
    per = 2
    chunks = kv * per
    width = columns // per
    own = rows // yz
    dma = pltpu.SemaphoreType.DMA
    return pl.pallas_call(
        functools.partial(project_kernel, gx, yz, chunks),
        out_shape=jax.ShapeDtypeStruct((own, kv * columns), jnp.float32),
        in_specs=[VMEM, VMEM, VMEM],
        out_specs=VMEM,
        scratch_shapes=[
            pltpu.VMEM((gx, rows_each, depth), jnp.bfloat16),
            pltpu.VMEM((8, rows), jnp.float32),
            pltpu.VMEM((yz - 1, 8, rows), jnp.float32),
            pltpu.VMEM((rows, depth), jnp.bfloat16),
            pltpu.VMEM((chunks, inner, outer, own, width), jnp.float32),
            pltpu.VMEM((chunks, inner - 1, outer, own, width), jnp.float32),
            pltpu.VMEM((chunks, outer, own, width), jnp.float32),
            pltpu.VMEM((chunks, outer - 1, own, width), jnp.float32),
            dma((gx - 1,)), dma((gx - 1,)),
            dma((yz - 1,)), dma((yz - 1,)),
            dma((chunks, inner - 1)), dma((chunks, inner - 1)),
            dma((chunks, outer - 1)), dma((chunks, outer - 1)),
        ],
        compiler_params=pltpu.CompilerParams(
            collective_id=0, has_side_effects=True, vmem_limit_bytes=10 * 2**20
        ),
        name="project",
    )(hidden, gain, weight)


CHUNK = 256


def attend_kernel(
    kv, lengths_ref, proj_ref, cos_ref, sin_ref, key_ref, value_ref, out_ref,
    values, queries, new_keys, new_values, scores, mixed, value_sem,
):
    rows = proj_ref.shape[0]
    heads = kv * QUERIES_PER_KEY
    span = CHUNK * kv

    def count(r):
        first = r // 2 * 2
        longer = jnp.maximum(lengths_ref[first], lengths_ref[first + 1])
        return (longer + CHUNK - 1) // CHUNK

    def copy_of(r, c):
        part = pl.ds(pl.multiple_of(c * span, span), span)
        return pltpu.make_async_copy(value_ref.at[r, part], values.at[r, part], value_sem.at[r, c])

    def begin(r, _):
        def each(c, _):
            copy_of(r, c).start()
            return 0

        return lax.fori_loop(0, count(r), each, 0)

    lax.fori_loop(0, rows, begin, 0)

    cosine, sine = cos_ref[...], sin_ref[...]
    for k in range(kv):
        for s in range(SLOTS):
            at = (k * SLOTS + s) * HEAD_SIZE
            x = proj_ref[:, at : at + HEAD_SIZE]
            if s <= QUERIES_PER_KEY:
                x = x * cosine + pltpu.roll(x, HEAD_SIZE // 2, 1) * sine
            x = x.astype(jnp.bfloat16).astype(jnp.float32)
            if s < QUERIES_PER_KEY:
                queries[:, k * QUERIES_PER_KEY + s, :] = x
            else:
                target = new_keys if s == QUERIES_PER_KEY else new_values
                for h in range(QUERIES_PER_KEY):
                    target[:, k * QUERIES_PER_KEY + h, :] = x

    factor = HEAD_SIZE ** (-0.5)
    column = lax.broadcasted_iota(jnp.int32, (heads, span), 1)
    head = lax.broadcasted_iota(jnp.int32, (heads, span), 0) // QUERIES_PER_KEY
    slot = column // kv
    slot = jnp.where(column - slot * kv == head, slot, 2**30)

    def pair(r, n):
        both = (0, 1)
        q32 = [queries[r + e] for e in both]
        lengths = [lengths_ref[r + e] for e in both]
        own = [jnp.sum(q32[e] * new_keys[r + e], axis=1, keepdims=True) * factor for e in both]
        largest = [None, None]
        for c in range(n):
            for e in both:
                s = lax.dot_general(
                    q32[e].astype(jnp.bfloat16),
                    key_ref[r + e, c * span : (c + 1) * span, :],
                    (((1,), (1,)), ((), ())),
                    preferred_element_type=jnp.float32,
                ) * factor
                s = jnp.where(slot < lengths[e] - c * CHUNK, s, -jnp.inf)
                scores[e, c] = s
                best = functools.reduce(
                    jnp.maximum, [s[:, t : t + 128] for t in range(0, span, 128)]
                )
                largest[e] = best if c == 0 else jnp.maximum(largest[e], best)
        largest = [
            jnp.maximum(jnp.max(largest[e], axis=1, keepdims=True), own[e]) for e in both
        ]
        own_weight = [jnp.exp(own[e] - largest[e]) for e in both]
        total = [None, None]
        for c in range(n):
            for e in both:
                w = jnp.exp(scores[e, c] - largest[e])
                scores[e, c] = w
                add = functools.reduce(
                    lambda x, y: x + y, [w[:, t : t + 128] for t in range(0, span, 128)]
                )
                total[e] = add if c == 0 else total[e] + add
        total = [jnp.sum(total[e], axis=1, keepdims=True) + own_weight[e] for e in both]
        inverse = [1.0 / total[e] for e in both]
        for c in range(n):
            for e in both:
                copy_of(r + e, c).wait()
        for e in both:
            acc = jnp.zeros((heads, HEAD_SIZE), jnp.float32)
            for c in range(n):
                probs = (scores[e, c] * inverse[e]).astype(jnp.bfloat16)
                acc = acc + jnp.dot(
                    probs,
                    values[r + e, c * span : (c + 1) * span, :],
                    preferred_element_type=jnp.float32,
                )
            own_prob = (own_weight[e] * inverse[e]).astype(jnp.bfloat16).astype(jnp.float32)
            mixed[r + e] = acc + own_prob * new_values[r + e]

    def step(p, _):
        r = p * 2
        needed = count(r)
        for n in range(1, scores.shape[1] + 1):
            pl.when(needed == n)(functools.partial(pair, r, n))
        return 0

    lax.fori_loop(0, rows // 2, step, 0)
    for h in range(heads):
        out_ref[:, h * HEAD_SIZE : (h + 1) * HEAD_SIZE] = mixed[:, h, :].astype(jnp.bfloat16)


def attend(lengths, proj, cosine, sine, keys, values, kv):
    rows, flat, _ = keys.shape
    heads = kv * QUERIES_PER_KEY
    chunks = flat // kv // CHUNK
    return pl.pallas_call(
        functools.partial(attend_kernel, kv),
        out_shape=jax.ShapeDtypeStruct((rows, heads * HEAD_SIZE), jnp.bfloat16),
        in_specs=[pl.BlockSpec(memory_space=pltpu.SMEM), VMEM, VMEM, VMEM, VMEM, ANY],
        out_specs=VMEM,
        scratch_shapes=[
            pltpu.VMEM((rows, flat, HEAD_SIZE), jnp.bfloat16),
            pltpu.VMEM((rows, heads, HEAD_SIZE), jnp.float32),
            pltpu.VMEM((rows, heads, HEAD_SIZE), jnp.float32),
            pltpu.VMEM((rows, heads, HEAD_SIZE), jnp.float32),
            pltpu.VMEM((2, chunks, heads, CHUNK * kv), jnp.float32),
            pltpu.VMEM((rows, heads, HEAD_SIZE), jnp.float32),
            pltpu.SemaphoreType.DMA((rows, chunks)),
        ],
        compiler_params=pltpu.CompilerParams(vmem_limit_bytes=22 * 2**20),
        name="attend",
    )(lengths, proj, cosine, sine, keys, values)


def output_kernel(
    gx, yz, chunks, heads_ref, weight_ref, out_ref,
    gathered, partial, partial_in,
    outer_send, outer_recv, inner_send, inner_recv, sum_send, sum_recv,
):
    outer, inner = factors(yz)
    g = lax.axis_index("gx")
    i = lax.axis_index("yz")
    a = i // inner
    b = lax.rem(i, inner)
    own_rows, depth = heads_ref.shape
    rows = own_rows * yz
    greet(
        [("gx", lax.rem(g + d, gx)) for d in range(1, gx)]
        + [("yz", lax.rem(a + d, outer) * inner + b) for d in range(1, outer)]
        + [("yz", a * inner + lax.rem(b + d, inner)) for d in range(1, inner)]
    )
    outer_copies, inner_copies = [], []
    for d in range(1, outer):
        outer_copies.append(
            start_copy(
                heads_ref, gathered.at[a, b], outer_send.at[d - 1], outer_recv.at[d - 1],
                "yz", lax.rem(a + d, outer) * inner + b,
            )
        )

    def relay(source, q, e):
        for d in range(1, inner):
            inner_copies.append(
                start_copy(
                    source, gathered.at[q, b], inner_send.at[e, d - 1], inner_recv.at[e, d - 1],
                    "yz", a * inner + lax.rem(b + d, inner),
                )
            )

    relay(heads_ref, a, 0)
    gathered[a, b] = heads_ref[...]
    for d in range(1, outer):
        outer_copies[d - 1].wait_recv()
        q = lax.rem(a + outer - d, outer)
        relay(gathered.at[q, b], q, d)
    for copy in inner_copies:
        copy.wait_recv()

    width = out_ref.shape[1] // chunks
    rows_each = rows // gx
    sums = []
    for c in range(chunks):
        part = jnp.dot(
            gathered[...].reshape(rows, depth),
            weight_ref[:, c * width : (c + 1) * width],
            preferred_element_type=jnp.float32,
        ).astype(jnp.bfloat16)
        for p in range(gx):
            partial[c, p] = part[p * rows_each : (p + 1) * rows_each]
        here = []
        for d in range(1, gx):
            p = lax.rem(g + d, gx)
            here.append(
                start_copy(
                    partial.at[c, p], partial_in.at[c, d - 1], sum_send.at[c, d - 1], sum_recv.at[c, d - 1], "gx", p
                )
            )
        sums.append(here)
    for c in range(chunks):
        value = partial[c, g].astype(jnp.float32)
        for d in range(1, gx):
            sums[c][d - 1].wait_recv()
            value = value + partial_in[c, d - 1].astype(jnp.float32)
        out_ref[:, c * width : (c + 1) * width] = value.astype(jnp.bfloat16)
    for copy in outer_copies + inner_copies:
        copy.wait_send()
    for here in sums:
        for copy in here:
            copy.wait_send()


def output(heads, weight, gx, yz):
    outer, inner = factors(yz)
    own, depth = heads.shape
    rows = own * yz
    columns = weight.shape[1]
    chunks = 3
    width = columns // chunks
    dma = pltpu.SemaphoreType.DMA
    return pl.pallas_call(
        functools.partial(output_kernel, gx, yz, chunks),
        out_shape=jax.ShapeDtypeStruct((rows // gx, columns), jnp.bfloat16),
        in_specs=[VMEM, VMEM],
        out_specs=VMEM,
        scratch_shapes=[
            pltpu.VMEM((outer, inner, own, depth), jnp.bfloat16),
            pltpu.VMEM((chunks, gx, rows // gx, width), jnp.bfloat16),
            pltpu.VMEM((chunks, gx - 1, rows // gx, width), jnp.bfloat16),
            dma((outer - 1,)), dma((outer - 1,)),
            dma((outer, inner - 1)), dma((outer, inner - 1)),
            dma((chunks, gx - 1)), dma((chunks, gx - 1)),
        ],
        compiler_params=pltpu.CompilerParams(
            collective_id=1, has_side_effects=True, vmem_limit_bytes=6 * 2**20
        ),
        name="output",
    )(heads, weight)


def body(
    hidden_in, norm_gain, query_key_value_weight, out_weight, key_cache, cached_value_rows, lengths
):
    gx, yz = lax.axis_size("gx"), lax.axis_size("yz")
    own, cached, kv, size = key_cache.shape
    proj = project(
        hidden_in, norm_gain.reshape(1, -1), jnp.transpose(query_key_value_weight, (1, 0, 2)), gx, yz
    )
    half = size // 2
    frequency = ROPE_BASE ** (-(jnp.arange(half, dtype=jnp.float32) * 2.0) / size)
    angles = lengths.astype(jnp.float32)[:, None] * frequency
    cosine, sine = jnp.cos(angles), jnp.sin(angles)
    heads = attend(
        lengths,
        proj,
        jnp.concatenate([cosine, cosine], axis=1),
        jnp.concatenate([-sine, sine], axis=1),
        key_cache.reshape(own, cached * kv, size),
        cached_value_rows.reshape(own, cached * kv, size),
        kv,
    )
    return output(heads, out_weight, gx, yz)


def solution(mesh):
    in_specs = (
        P("gx", "yz"),
        P("yz"),
        P("yz", "gx", None),
        P("gx", "yz"),
        P("yz", None, "gx", None),
        P("yz", None, "gx", None),
        P("yz"),
    )
    out_specs = P("gx", "yz")
    return jax.shard_map(body, mesh=mesh, in_specs=in_specs, out_specs=out_specs, check_vma=False)
```
